256 devices in a mesh: ctx: 32 (over x, z), tp: 8 (over y, core).
Axes of the slice: x: 4, y: 4, z: 8, core: 2. Of those that a mesh axis runs over, the one named last changes fastest.
Arguments:
- queries: bfloat16 [16384, 8192], P('ctx', 'tp'), may hold values from -96 to 96
- keys: bfloat16 [16384, 1024], P(('ctx', 'tp')), may hold values from -6 to 6
- values: bfloat16 [16384, 1024], P(('ctx', 'tp')), may hold values from -6 to 6
- block_bound: int32 [64], replicated, may hold values from 0 to 256, as said below
- block_home: int32 [64], replicated, may hold values from 0 to 63, as said below
- pair_query: int32 [32, 32], P('ctx'), may hold values from -1 to 63, as said below
- pair_key: int32 [32, 32], P('ctx'), may hold values from -1 to 63, as said below
Outputs:
- attended: bfloat16 [16384, 8192], P('ctx', 'tp')
The draws below stay inside these ranges and needn't reach their ends.
Inputs may be any that keep to these rules, and one draw needn't show every extreme that they name: `block_bound`: 256 marks a block without a document start; each aligned run of 8 logical blocks holds exactly one block with a value below 256. `block_home`: a permutation of 0 to 63. `pair_query`: over all workers, the listed pairs are exactly the pairs (q, k) of logical blocks with k <= q such that some token of q may see some token of k, each once; k >= q - 2 * 8 + 1; the pairs of worker w have query blocks whose owner is w - j mod 32 with 0 <= j < 4; the listed slots of a worker come first and the others hold -1. `pair_key`: the key block of the same slot, -1 exactly where pair_query is -1.
All inputs are finite; a program needn't handle non-finite values.
Results may differ from the reference program's by a relative error of at most 0.0048.
Values may be sent and summed in bfloat16 or wider, within the bound.
No kernel may reach another device: no remote copies, remote signals or barrier semaphores. Data moves between devices by JAX's collectives and lax.ppermute only.
A program may use at most 64 MiB of HBM per device.

```python
import jax
import jax.numpy as jnp
from jax import lax

Q_HEADS = 64
KV_HEADS = 8
HEAD_DIM = 128
BLK = 256
BPD = 2
DOCW = 8
HELP = 4
NB = 64
TOKENS = 16384
PAIRS_DEV = 32
N_CTX = 32


def layout(key):
    first_key, second_key, third_key = jax.random.split(key, 3)
    windows = NB // DOCW
    chosen = jax.random.randint(first_key, (windows,), 0, DOCW).astype(jnp.int32)
    start_row = jax.random.randint(second_key, (windows,), 0, BLK).astype(jnp.int32)
    start_block = jnp.arange(windows, dtype=jnp.int32) * DOCW + chosen
    bounds = jnp.full((NB,), BLK, jnp.int32).at[start_block].set(start_row)
    home = jax.random.permutation(third_key, NB).astype(jnp.int32)
    return (bounds, home)


def assign(key):
    bounds, home = layout(key)
    blocks = jnp.arange(NB, dtype=jnp.int32)
    has_start = (bounds < BLK).astype(jnp.int32)
    counts = jnp.cumsum(has_start)
    query_grid = jnp.broadcast_to(blocks[:, None], (NB, NB))
    key_grid = jnp.broadcast_to(blocks[None, :], (NB, NB))
    between = counts[jnp.maximum(query_grid - 1, 0)] - counts[key_grid]
    needed = (key_grid == query_grid) | (key_grid < query_grid) & (between == 0) & (bounds[query_grid] != 0)
    query_flat = query_grid.reshape(-1)
    key_flat = key_grid.reshape(-1)
    needed_flat = needed.reshape(-1)
    owner_of = home[query_flat] // BPD
    order_key = owner_of * NB * NB + query_flat * NB + key_flat
    before_me = (owner_of[:, None] == owner_of[None, :]) & needed_flat[None, :] & (order_key[None, :] < order_key[:, None])
    rank_in = jnp.sum(before_me.astype(jnp.int32), axis=1)
    offset = rank_in % HELP
    worker = (owner_of + offset) % N_CTX
    worker_key = offset * NB * NB + rank_in
    ahead = (worker[:, None] == worker[None, :]) & needed_flat[None, :] & (worker_key[None, :] < worker_key[:, None])
    slot_in = jnp.sum(ahead.astype(jnp.int32), axis=1)
    worker_row = jnp.where(needed_flat, worker, N_CTX)
    query_list = jnp.full((N_CTX, PAIRS_DEV), -1, jnp.int32).at[worker_row, slot_in].set(query_flat, mode='drop')
    key_list = jnp.full((N_CTX, PAIRS_DEV), -1, jnp.int32).at[worker_row, slot_in].set(key_flat, mode='drop')
    return (query_list, key_list)


def draw_block_bound(key, part):
    return layout(key)[0]


def draw_block_home(key, part):
    return layout(key)[1]


def draw_pair_query(key, part):
    return assign(key)[0]


def draw_pair_key(key, part):
    return assign(key)[1]


def draw_keys(key, part):
    key = jax.random.fold_in(key, 5)
    private = jnp.clip(jax.random.normal(key, (TOKENS, KV_HEADS * HEAD_DIM), jnp.float32), -6.0, 6.0)
    return private.astype(jnp.bfloat16)


def draw_queries(key, part):
    key = jax.random.fold_in(key, 7)
    first_key = jax.random.fold_in(key, 0)
    private = jnp.clip(jax.random.normal(first_key, (TOKENS, Q_HEADS * HEAD_DIM), jnp.float32), -6.0, 6.0)
    return private.astype(jnp.bfloat16)


def levels(rng, shape, cuts, smallest, high):
    loudness, own = 1.0, jax.random.fold_in(rng, 6)
    for dim, shards_of in cuts:
        steps = jnp.exp(jax.random.uniform(jax.random.fold_in(own, dim), (shards_of,), jnp.float32, smallest / len(cuts), high / len(cuts)))
        loudness = loudness * jnp.repeat(steps, shape[dim] // shards_of).reshape([-1 if axis == dim else 1 for axis in range(len(shape))])
    return loudness


def noise(stream_key, extent, width, most, pieces=(), kind=jnp.bfloat16):
    drawn = jax.random.normal(stream_key, extent, jnp.float32) * width
    if len(pieces) > 0:
        drawn = levels(stream_key, extent, pieces, -0.22, 0.18) * drawn
    return jnp.clip(drawn, min=-most, max=most).astype(kind)


def setup_inputs(seed: int = 0) -> dict:
    streams_of = jax.random.split(jax.random.key(seed), 8)
    return {
        "queries": draw_queries(jax.random.fold_in(streams_of[7], 71), 0),
        "keys": draw_keys(jax.random.fold_in(streams_of[7], 71), 0),
        "values": noise(streams_of[2], (TOKENS, KV_HEADS * HEAD_DIM), 1.0, 6.0, ((0, 256),)),
        "block_bound": draw_block_bound(jax.random.fold_in(streams_of[7], 71), 0),
        "block_home": draw_block_home(jax.random.fold_in(streams_of[7], 71), 0),
        "pair_query": draw_pair_query(jax.random.fold_in(streams_of[7], 71), 0),
        "pair_key": draw_pair_key(jax.random.fold_in(streams_of[7], 71), 0),
    }


NEG = -1.0e30


def token_docs(block_bound):
    starts = (block_bound < BLK).astype(jnp.int32)
    earlier = jnp.cumsum(starts) - starts
    row_index = jnp.arange(BLK, dtype=jnp.int32)
    return earlier[:, None] + (row_index[None, :] >= block_bound[:, None]).astype(jnp.int32)


def pair_stats(query_tile, key_tile, value_tile, query_block, key_block, doc_ids):
    scores = jnp.einsum("qkgd,pkd->qkgp", query_tile.astype(jnp.float32), key_tile.astype(jnp.float32)) * (HEAD_DIM ** -0.5)
    query_pos = query_block * BLK + jnp.arange(BLK, dtype=jnp.int32)
    key_pos = key_block * BLK + jnp.arange(BLK, dtype=jnp.int32)
    allowed = (doc_ids[query_block][:, None] == doc_ids[key_block][None, :]) & (key_pos[None, :] <= query_pos[:, None])
    allowed = allowed[:, None, None, :]
    scores = jnp.where(allowed, scores, NEG)
    maxima = jnp.max(scores, axis=-1)
    weights = jnp.where(allowed, jnp.exp(scores - maxima[..., None]), 0.0)
    totals = jnp.sum(weights, axis=-1)
    rounded = lax.optimization_barrier(weights.astype(jnp.bfloat16)).astype(jnp.float32)
    weighted = jnp.einsum("qkgp,pkd->qkgd", rounded, value_tile.astype(jnp.float32))
    return maxima, totals, weighted


def combine(running, fresh):
    largest = jnp.maximum(running[0], fresh[0])
    scale_old = jnp.exp(running[0] - largest)
    scale_new = jnp.exp(fresh[0] - largest)
    totals = running[1] * scale_old + fresh[1] * scale_new
    weighted = running[2] * scale_old[..., None] + fresh[2] * scale_new[..., None]
    return largest, totals, weighted


def finish(maxima, totals, weighted):
    divisor = jnp.where(totals > 0, totals, 1.0)
    partial_value = jnp.where(totals[..., None] > 0, weighted / divisor[..., None], 0.0).astype(jnp.bfloat16)
    logsum = jnp.where(totals > 0, maxima + jnp.log(divisor), NEG)
    return partial_value, logsum


def reference(queries, keys, values, block_bound, block_home, pair_query, pair_key):
    group_size = Q_HEADS // KV_HEADS
    query_blocks = queries.reshape(NB, BLK, KV_HEADS, group_size, HEAD_DIM)[block_home]
    key_blocks = keys.reshape(NB, BLK, KV_HEADS, HEAD_DIM)[block_home]
    value_blocks = values.reshape(NB, BLK, KV_HEADS, HEAD_DIM)[block_home]
    doc_ids = token_docs(block_bound)
    owner_of = block_home // BPD
    workers = jnp.broadcast_to(jnp.arange(N_CTX, dtype=jnp.int32)[:, None], pair_query.shape).reshape(-1)
    query_flat = pair_query.reshape(-1)
    key_flat = pair_key.reshape(-1)
    listed_flag = query_flat >= 0
    offsets = (workers - owner_of[jnp.maximum(query_flat, 0)]) % N_CTX
    offset_table = jnp.full((NB, NB), -1, jnp.int32).at[
        jnp.where(listed_flag, query_flat, NB), jnp.maximum(key_flat, 0)].set(offsets, mode="drop")
    reach_back = 2 * DOCW

    def one_block(query_block):
        query_tile = query_blocks[query_block]
        partials = []
        logsums = []
        for offset in range(HELP):
            def visit_back(back, running):
                key_block = query_block - back
                key_clamped = jnp.maximum(key_block, 0).astype(jnp.int32)
                listed = (key_block >= 0) & (offset_table[query_block, key_clamped] == offset)

                def compute(state):
                    return combine(state, pair_stats(query_tile, key_blocks[key_clamped], value_blocks[key_clamped], query_block, key_clamped, doc_ids))

                return lax.cond(listed, compute, lambda state: state, running)

            initial = (jnp.full((BLK, KV_HEADS, group_size), NEG, jnp.float32),
                       jnp.zeros((BLK, KV_HEADS, group_size), jnp.float32),
                       jnp.zeros((BLK, KV_HEADS, group_size, HEAD_DIM), jnp.float32))
            maxima, totals, weighted = lax.fori_loop(0, reach_back, visit_back, initial)
            partial_value, logsum = finish(maxima, totals, weighted)
            partials.append(partial_value)
            logsums.append(logsum)
        stacked = lax.optimization_barrier(jnp.stack(partials)).astype(jnp.float32)
        logsums = jnp.stack(logsums)
        largest = jnp.max(logsums, axis=0)
        weight = jnp.exp(logsums - largest)
        denominator = jnp.sum(weight, axis=0)
        merged = jnp.sum(weight[..., None] * stacked, axis=0) / denominator[..., None]
        return merged.astype(jnp.bfloat16)

    result = lax.map(one_block, jnp.arange(NB, dtype=jnp.int32))
    stored = jnp.zeros_like(result).at[block_home].set(result)
    return stored.reshape(TOKENS, Q_HEADS * HEAD_DIM)
```

```python
import functools

import jax
import jax.numpy as jnp
from jax import lax
from jax.experimental import pallas as pl
from jax.experimental.pallas import tpu as pltpu
from jax.sharding import PartitionSpec as P

HEAD_DIM = 128
BLK = 256
BPD = 2
NB = 64
GROUP = 8
NX, NZ = 4, 8
BACK = 16
NEG = -1e30
SCALE = HEAD_DIM ** (-0.5) * 1.4426950408889634


def moved(block, dx, dz):
    route = [
        (x * NZ + z, (x + dx) % NX * NZ + (z + dz) % NZ)
        for x in range(NX)
        for z in range(NZ)
    ]
    return lax.ppermute(block, "ctx", route)


def chain(block, dx, dz, steps):
    out = []
    for _ in range(steps):
        block = moved(block, dx, dz)
        out.append(block)
    return out


def gather_blocks(own):
    up = chain(own, 0, 1, 4)
    down = chain(own, 0, -1, 3)
    right = chain(own, 1, 0, 2)
    left = chain(own, -1, 0, 1)
    both = lambda dx, dz: [(dx, dz, 0), (dx, dz, 1)]
    pieces = [(own, both(0, 0))]
    pieces += [(v, both(0, -i - 1)) for i, v in enumerate(up)]
    pieces += [(v, both(0, i + 1)) for i, v in enumerate(down)]
    pieces += [(v, both(-i - 1, 0)) for i, v in enumerate(right)]
    pieces += [(v, both(i + 1, 0)) for i, v in enumerate(left)]
    first = jnp.concatenate([right[0][:1], left[0][:1], right[1][:1]])
    for i, v in enumerate(chain(first, 0, 1, 3)):
        pieces.append((v, [(-1, -i - 1, 0), (1, -i - 1, 0), (-2, -i - 1, 0)]))
    for i, v in enumerate(chain(first, 0, -1, 4)):
        pieces.append((v, [(-1, i + 1, 0), (1, i + 1, 0), (-2, i + 1, 0)]))
    near = jnp.concatenate([up[0][1:], down[0][1:], up[1][1:], down[1][1:]])
    far = jnp.concatenate([up[2][1:], down[2][1:], up[3][1:]])
    for lump, dzs, n_right, n_left in ((near, (-1, 1, -2, 2), 1, 2), (far, (-3, 3, -4), 2, 1)):
        for i, v in enumerate(chain(lump, 1, 0, n_right)):
            pieces.append((v, [(-i - 1, dz, 1) for dz in dzs]))
        for i, v in enumerate(chain(lump, -1, 0, n_left)):
            pieces.append((v, [(i + 1, dz, 1) for dz in dzs]))
    return pieces


def attend_kernel(places, home_ref, bound_ref, q_ref, *refs):
    n_bufs = len(places)
    bufs, (o_ref, kv, m_ref, l_ref, acc_ref, inv, lid, cnt, sem) = refs[:n_bufs], refs[n_bufs:]
    me = lax.axis_index("ctx")
    my_x, my_z = me // NZ, me % NZ

    @pl.loop(0, NB)
    def _(b):
        inv[home_ref[b]] = b

    blocks, firsts = [], []
    for qb in range(BPD):
        block = inv[me * BPD + qb]
        first = lax.fori_loop(
            0,
            BACK,
            lambda i, f, block=block: jnp.where(
                (block - 1 - i >= 0) & (f < 0) & (bound_ref[jnp.maximum(block - 1 - i, 0)] < BLK),
                block - 1 - i,
                f,
            ),
            jnp.int32(-1),
        )
        first = jnp.where(bound_ref[block] == 0, block, jnp.maximum(first, 0))
        blocks.append(block)
        firsts.append(first)
        cnt[qb] = 0

    def fetch(src, qb, slot):
        return pltpu.make_async_copy(src, kv.at[qb, slot], sem.at[qb, slot])

    for buf, spots in zip(bufs, places):
        for i, (dx, dz, b) in enumerate(spots):
            stored = ((my_x + dx + NX) % NX * NZ + (my_z + dz + NZ) % NZ) * BPD + b
            logical = inv[stored]
            for qb in range(BPD):
                if (dx, dz) == (0, 0):
                    continue

                @pl.when((logical >= firsts[qb]) & (logical < blocks[qb]))
                def _():
                    slot = cnt[qb] + 1
                    lid[qb, slot] = logical
                    cnt[qb] = slot
                    fetch(buf.at[i], qb, slot).start()

    for qb in range(BPD):
        other = blocks[1 - qb]
        fetch(bufs[0].at[qb], qb, 0).start()

        @pl.when((other >= firsts[qb]) & (other < blocks[qb]))
        def _():
            slot = cnt[qb] + 1
            lid[qb, slot] = other
            cnt[qb] = slot
            fetch(bufs[0].at[1 - qb], qb, slot).start()

    for qb in range(BPD):
        block, first = blocks[qb], firsts[qb]
        rows = pl.ds(qb * BLK, BLK)
        bound = bound_ref[block]
        first_bound = bound_ref[first]
        doc_start = first * BLK + jnp.where((first < block) & (first_bound < BLK), first_bound, 0)
        row = lax.broadcasted_iota(jnp.int32, (BLK, 1), 0)
        low = jnp.where(row < bound, doc_start, block * BLK + bound)
        high = row + block * BLK

        def allowed(ids):
            col = lax.broadcasted_iota(jnp.int32, (1, BLK), 1)
            at = jnp.concatenate([col + i * BLK for i in ids], 1)
            return (at >= low) & (at <= high)

        def step(slots, ids, masked, fresh):
            keys = jnp.concatenate([kv[qb, s, :, 0].reshape(BLK, HEAD_DIM) for s in slots])
            vals = jnp.concatenate([kv[qb, s, :, 1].reshape(BLK, HEAD_DIM) for s in slots])
            mask = allowed(ids) if masked else None
            for h in range(GROUP):
                q = q_ref[rows, h * HEAD_DIM : (h + 1) * HEAD_DIM]
                s = lax.dot_general(
                    q, keys, (((1,), (1,)), ((), ())), preferred_element_type=jnp.float32
                )
                s = s * SCALE
                if masked:
                    s = jnp.where(mask, s, NEG)
                top = jnp.max(s, axis=1, keepdims=True)
                if not fresh:
                    old = m_ref[h]
                    top = jnp.maximum(old, top)
                    fade = jnp.exp2(old - top)
                    w = jnp.exp2(s - top[:, :1])
                else:
                    top = jnp.broadcast_to(top, (BLK, HEAD_DIM))
                    w = jnp.exp2(s - top[:, :1])
                total = jnp.sum(w, axis=1, keepdims=True)
                pv = jnp.dot(w.astype(jnp.bfloat16), vals, preferred_element_type=jnp.float32)
                m_ref[h] = top
                if fresh:
                    l_ref[h] = jnp.broadcast_to(total, (BLK, HEAD_DIM))
                    acc_ref[h] = pv
                else:
                    l_ref[h] = l_ref[h] * fade + total
                    acc_ref[h] = acc_ref[h] * fade + pv

        def arrived(slot):
            fetch(bufs[0].at[qb], qb, slot).wait()

        arrived(0)
        step([0], [block], True, True)
        seen = cnt[qb]

        @pl.loop(0, seen // 2)
        def _(c):
            slots = [1 + 2 * c, 2 + 2 * c]
            for s in slots:
                arrived(s)
            ids = [lid[qb, s] for s in slots]
            edge = (bound < BLK) | (ids[0] == first) | (ids[1] == first)

            @pl.when(edge)
            def _():
                step(slots, ids, True, False)

            @pl.when(jnp.logical_not(edge))
            def _():
                step(slots, ids, False, False)

        @pl.when(seen % 2 == 1)
        def _():
            arrived(seen)
            step([seen], [lid[qb, seen]], True, False)

        for h in range(GROUP):
            o_ref[rows, h * HEAD_DIM : (h + 1) * HEAD_DIM] = (acc_ref[h] / l_ref[h]).astype(
                o_ref.dtype
            )


def attend(queries, block_bound, block_home, pieces):
    bufs = [v for v, _ in pieces]
    places = [p for _, p in pieces]
    smem = pl.BlockSpec(memory_space=pltpu.SMEM)
    vmem = pl.BlockSpec(memory_space=pltpu.VMEM)
    stat = pltpu.VMEM((GROUP, BLK, HEAD_DIM), jnp.float32)
    return pl.pallas_call(
        functools.partial(attend_kernel, places),
        out_shape=jax.ShapeDtypeStruct(queries.shape, queries.dtype),
        in_specs=[smem, smem, vmem] + [pl.BlockSpec(memory_space=pl.ANY)] * len(bufs),
        out_specs=vmem,
        scratch_shapes=[
            pltpu.VMEM((BPD, BACK, 4, 2, 64, HEAD_DIM), jnp.bfloat16),
            stat,
            stat,
            stat,
            pltpu.SMEM((NB,), jnp.int32),
            pltpu.SMEM((BPD, BACK), jnp.int32),
            pltpu.SMEM((BPD,), jnp.int32),
            pltpu.SemaphoreType.DMA((BPD, BACK)),
        ],
        compiler_params=pltpu.CompilerParams(vmem_limit_bytes=24 * 1024 * 1024),
    )(block_home, block_bound, queries, *bufs)


def on_device(queries, keys, values, block_bound, block_home, pair_query, pair_key):
    rows = keys.shape[0]
    heads = keys.shape[1] // HEAD_DIM
    out = jnp.stack([keys, values]).reshape(2, rows, heads, HEAD_DIM).transpose(2, 0, 1, 3)
    own = lax.all_to_all(out, "tp", split_axis=0, concat_axis=0, tiled=True)
    own = own.reshape(BPD, heads // BPD, 2, rows, HEAD_DIM)
    return attend(queries, block_bound, block_home, gather_blocks(own))


def solution(mesh):
    in_specs = (
        P("ctx", "tp"),
        P(("ctx", "tp"), None),
        P(("ctx", "tp"), None),
        P(),
        P(),
        P("ctx", None),
        P("ctx", None),
    )
    return jax.shard_map(
        on_device, mesh=mesh, in_specs=in_specs, out_specs=P("ctx", "tp"), check_vma=False
    )
```

```python
import functools

import jax
import jax.numpy as jnp
from jax import lax
from jax.experimental import pallas as pl
from jax.experimental.pallas import tpu as pltpu
from jax.sharding import PartitionSpec as P

HEAD_DIM = 128
BLK = 256
BPD = 2
NB = 64
GROUP = 8
NX, NZ = 4, 8
BACK = 16
NEG = -1e30
RT = 128
UNROLL = 8
COST = 300 * 1000 * 1000
SCALE = HEAD_DIM ** (-0.5) * 1.4426950408889634


def moved(block, dx, dz):
    route = [
        (x * NZ + z, (x + dx) % NX * NZ + (z + dz) % NZ)
        for x in range(NX)
        for z in range(NZ)
    ]
    return lax.ppermute(block, "ctx", route)


def chain(block, dx, dz, steps):
    out = []
    for _ in range(steps):
        block = moved(block, dx, dz)
        out.append(block)
    return out


def gather_blocks(own):
    up = chain(own, 0, 1, 4)
    down = chain(own, 0, -1, 3)
    right = chain(own, 1, 0, 2)
    left = chain(own, -1, 0, 1)
    both = lambda dx, dz: [(dx, dz, 0), (dx, dz, 1)]
    early = [(own, both(0, 0))]
    early += [(v, both(0, -i - 1)) for i, v in enumerate(up)]
    early += [(v, both(0, i + 1)) for i, v in enumerate(down)]
    early += [(v, both(-i - 1, 0)) for i, v in enumerate(right)]
    early += [(v, both(i + 1, 0)) for i, v in enumerate(left)]
    first = jnp.concatenate([right[0][:1], left[0][:1], right[1][:1]])
    ahead = chain(first, 0, 1, 3)
    back = chain(first, 0, -1, 4)
    ahead = [(v, [(dx, -i - 1, 0) for dx in (-1, 1, -2)]) for i, v in enumerate(ahead)]
    back = [(v, [(dx, i + 1, 0) for dx in (-1, 1, -2)]) for i, v in enumerate(back)]
    middle, late = ahead[:-1] + back[:-1], [ahead[-1], back[-1]]
    near = jnp.concatenate([up[0][1:], down[0][1:], up[1][1:], down[1][1:]])
    far = jnp.concatenate([up[2][1:], down[2][1:], up[3][1:]])
    for lump, dzs, n_right, n_left in ((near, (-1, 1, -2, 2), 1, 2), (far, (-3, 3, -4), 2, 1)):
        for step, n in ((1, n_right), (-1, n_left)):
            for i, v in enumerate(chain(lump, step, 0, n)):
                (middle if i == 0 else late).append((v, [(-step * (i + 1), dz, 1) for dz in dzs]))
    return early, middle, late


def attend_kernel(places, opening, closing, unroll, home_ref, bound_ref, q_ref, *refs):
    n_bufs = len(places)
    n_in = n_bufs if opening else n_bufs + 3
    bufs, old, rest = refs[:n_bufs], refs[n_bufs:n_in], refs[n_in:]
    if closing:
        (o_ref, m_ref, l_ref, acc_ref), rest = rest[:4], rest[4:]
    else:
        (m_ref, l_ref, acc_ref), rest = rest[:3], rest[3:]
    kv, inv, lid, cnt, span, sem = rest
    if opening:
        m_old = l_old = acc_old = None
    else:
        m_old, l_old, acc_old = old
    me = lax.axis_index("ctx")
    my_x, my_z = me // NZ, me % NZ

    @pl.loop(0, NB)
    def _(b):
        inv[home_ref[b]] = b

    for qb in range(BPD):
        block = inv[me * BPD + qb]
        first = lax.fori_loop(
            0,
            BACK,
            lambda i, f, block=block: jnp.where(
                (block - 1 - i >= 0) & (f < 0) & (bound_ref[jnp.maximum(block - 1 - i, 0)] < BLK),
                block - 1 - i,
                f,
            ),
            jnp.int32(-1),
        )
        span[qb, 0] = block
        span[qb, 1] = jnp.where(bound_ref[block] == 0, block, jnp.maximum(first, 0))
        cnt[qb] = 0
    blocks = [span[qb, 0] for qb in range(BPD)]
    firsts = [span[qb, 1] for qb in range(BPD)]

    def fetch(src, qb, slot):
        return pltpu.make_async_copy(src, kv.at[qb, slot], sem.at[qb, slot])

    def list_slot(qb, logical):
        slot = cnt[qb]
        lid[qb, slot] = logical
        cnt[qb] = slot + 1
        return slot

    if opening:
        for qb in range(BPD):
            fetch(bufs[0].at[qb], qb, list_slot(qb, blocks[qb])).start()

    for buf, spots in zip(bufs, places):
        for i, (dx, dz, b) in enumerate(spots):
            stored = ((my_x + dx + NX) % NX * NZ + (my_z + dz + NZ) % NZ) * BPD + b
            logical = inv[stored]
            for qb in range(BPD):

                @pl.when((logical >= firsts[qb]) & (logical < blocks[qb]))
                def _():
                    fetch(buf.at[i], qb, list_slot(qb, logical)).start()

    @pl.loop(0, BPD)
    def _(qb):
        block, first = span[qb, 0], span[qb, 1]
        top_row = pl.multiple_of(qb * BLK, BLK)
        bound = bound_ref[block]
        first_bound = bound_ref[first]
        doc_start = first * BLK + jnp.where((first < block) & (first_bound < BLK), first_bound, 0)
        row = lax.broadcasted_iota(jnp.int32, (BLK, 1), 0)
        low = jnp.where(row < bound, doc_start, block * BLK + bound)
        high = row + block * BLK

        def allowed(ids):
            col = lax.broadcasted_iota(jnp.int32, (1, BLK), 1)
            at = jnp.concatenate([col + i * BLK for i in ids], 1)
            return (at >= low) & (at <= high)

        def step(slots, ids, masked, fresh):
            keys = jnp.concatenate([kv[qb, s, :, 0].reshape(BLK, HEAD_DIM) for s in slots])
            vals = jnp.concatenate([kv[qb, s, :, 1].reshape(BLK, HEAD_DIM) for s in slots])
            n = len(slots) * BLK // HEAD_DIM
            vals = jnp.concatenate([vals, jnp.ones_like(vals)], 1)
            mask = allowed(ids) if masked else None

            def one_head(h):
                lanes = pl.ds(pl.multiple_of(h * HEAD_DIM, HEAD_DIM), HEAD_DIM)
                for r in range(0, BLK, RT):
                    at = (qb * GROUP + h, pl.ds(r, RT))
                    q = q_ref[pl.ds(top_row + r, RT), lanes]
                    s = lax.dot_general(
                        q, keys, (((1,), (1,)), ((), ())), preferred_element_type=jnp.float32
                    )
                    s = s * SCALE
                    if masked:
                        s = jnp.where(mask[r : r + RT], s, NEG)
                    top = jnp.max(s, axis=1, keepdims=True)
                    if fresh:
                        top = jnp.broadcast_to(top, (RT, HEAD_DIM))
                    else:
                        before = m_ref[at]
                        top = jnp.maximum(before, top)
                        fade = jnp.exp2(before - top)
                    w = jnp.exp2(s - jnp.concatenate([top] * n, 1))
                    pv = jnp.dot(
                        w.astype(jnp.bfloat16), vals, preferred_element_type=jnp.float32
                    )
                    m_ref[at] = top
                    if fresh:
                        l_ref[at] = pv[:, HEAD_DIM:]
                        acc_ref[at] = pv[:, :HEAD_DIM]
                    else:
                        l_ref[at] = l_ref[at] * fade + pv[:, HEAD_DIM:]
                        acc_ref[at] = acc_ref[at] * fade + pv[:, :HEAD_DIM]

            if unroll == GROUP:
                for h in range(GROUP):
                    one_head(h)
            else:

                @pl.loop(0, GROUP // unroll)
                def _(g):
                    for i in range(unroll):
                        one_head(g * unroll + i)

        def arrived(slot):
            fetch(bufs[0].at[0], qb, slot).wait()

        if opening:
            arrived(0)
            step([0], [block], True, True)
            base = 1
        else:
            mine = pl.ds(qb * GROUP, GROUP)
            m_ref[mine] = m_old[mine]
            l_ref[mine] = l_old[mine]
            acc_ref[mine] = acc_old[mine]
            base = 0
        seen = cnt[qb] - base

        @pl.loop(0, seen // 2)
        def _(c):
            slots = [base + 2 * c, base + 1 + 2 * c]
            for s in slots:
                arrived(s)
            ids = [lid[qb, s] for s in slots]
            edge = (bound < BLK) | (ids[0] == first) | (ids[1] == first)

            @pl.when(edge)
            def _():
                step(slots, ids, True, False)

            @pl.when(jnp.logical_not(edge))
            def _():
                step(slots, ids, False, False)

        @pl.when(seen % 2 == 1)
        def _():
            last = base + seen - 1
            arrived(last)
            step([last], [lid[qb, last]], True, False)

        if closing:
            for h in range(GROUP):
                at = qb * GROUP + h
                o_ref[pl.ds(top_row, BLK), h * HEAD_DIM : (h + 1) * HEAD_DIM] = (
                    acc_ref[at] / l_ref[at]
                ).astype(o_ref.dtype)


def attend(queries, block_bound, block_home, pieces, state=(), closing=True, unroll=UNROLL):
    bufs = [v for v, _ in pieces]
    places = [p for _, p in pieces]
    smem = pl.BlockSpec(memory_space=pltpu.SMEM)
    vmem = pl.BlockSpec(memory_space=pltpu.VMEM)
    stat = (BPD * GROUP, BLK, HEAD_DIM)
    n_blocks = sum(len(p) for p in places)
    if closing:
        out_shape = jax.ShapeDtypeStruct(queries.shape, queries.dtype)
        kept = [pltpu.VMEM(stat, jnp.float32)] * 3
    else:
        out_shape = [jax.ShapeDtypeStruct(stat, jnp.float32)] * 3
        kept = []
    return pl.pallas_call(
        functools.partial(attend_kernel, places, not state, closing, unroll),
        out_shape=out_shape,
        in_specs=[smem, smem, vmem]
        + [pl.BlockSpec(memory_space=pl.ANY)] * len(bufs)
        + [vmem] * len(state),
        out_specs=vmem if closing else [vmem] * 3,
        scratch_shapes=kept
        + [
            pltpu.VMEM((BPD, BACK, 4, 2, 64, HEAD_DIM), jnp.bfloat16),
            pltpu.SMEM((NB,), jnp.int32),
            pltpu.SMEM((BPD, BACK), jnp.int32),
            pltpu.SMEM((BPD,), jnp.int32),
            pltpu.SMEM((BPD, 2), jnp.int32),
            pltpu.SemaphoreType.DMA((BPD, BACK)),
        ],
        cost_estimate=pl.CostEstimate(
            flops=n_blocks * COST, bytes_accessed=8 * 1024 * 1024, transcendentals=0
        ),
        compiler_params=pltpu.CompilerParams(vmem_limit_bytes=32 * 1024 * 1024),
    )(block_home, block_bound, queries, *bufs, *state)


def on_device(queries, keys, values, block_bound, block_home, pair_query, pair_key):
    rows = keys.shape[0]
    heads = keys.shape[1] // HEAD_DIM
    out = jnp.stack([keys, values]).reshape(2, rows, heads, HEAD_DIM).transpose(2, 0, 1, 3)
    own = lax.all_to_all(out, "tp", split_axis=0, concat_axis=0, tiled=True)
    own = own.reshape(BPD, heads // BPD, 2, rows, HEAD_DIM)
    args = (queries, block_bound, block_home)
    early, middle, late = gather_blocks(own)
    state = attend(*args, early + middle, closing=False)
    return attend(*args, late, state)


def solution(mesh):
    in_specs = (
        P("ctx", "tp"),
        P(("ctx", "tp"), None),
        P(("ctx", "tp"), None),
        P(),
        P(),
        P("ctx", None),
        P("ctx", None),
    )
    return jax.shard_map(
        on_device, mesh=mesh, in_specs=in_specs, out_specs=P("ctx", "tp"), check_vma=False
    )
```

```python
import functools

import jax
import jax.numpy as jnp
from jax import lax
from jax.experimental import pallas as pl
from jax.experimental.pallas import tpu as pltpu
from jax.sharding import PartitionSpec as P

HEAD_DIM = 128
BLK = 256
BPD = 2
NB = 64
GROUP = 8
NX, NZ = 4, 8
BACK = 16
NEG = -1e30
RT = 128
UNROLL = 8
COST = 300 * 1000 * 1000
SCALE = HEAD_DIM ** (-0.5) * 1.4426950408889634


def moved(block, dx, dz):
    route = [
        (x * NZ + z, (x + dx) % NX * NZ + (z + dz) % NZ)
        for x in range(NX)
        for z in range(NZ)
    ]
    return lax.ppermute(block, "ctx", route)


def chain(block, dx, dz, steps):
    out = []
    for _ in range(steps):
        block = moved(block, dx, dz)
        out.append(block)
    return out


def gather_blocks(own, work):
    up = chain(own, 0, 1, 4)
    down = chain(own, 0, -1, 3)
    right = chain(own, 1, 0, 2)
    left = chain(own, -1, 0, 1)
    both = lambda dx, dz: [(dx, dz, 0), (dx, dz, 1)]
    early = [(own, both(0, 0))]
    early += [(v, both(0, -i - 1)) for i, v in enumerate(up[:3])]
    early += [(v, both(0, i + 1)) for i, v in enumerate(down)]
    early += [(v, both(-i - 1, 0)) for i, v in enumerate(right)]
    early += [(v, both(i + 1, 0)) for i, v in enumerate(left)]
    first = jnp.concatenate([right[0][:1], left[0][:1], right[1][:1]])
    ahead = chain(first, 0, 1, 3)
    back = chain(first, 0, -1, 4)
    ahead = [(v, [(dx, -i - 1, 0) for dx in (-1, 1, -2)]) for i, v in enumerate(ahead)]
    back = [(v, [(dx, i + 1, 0) for dx in (-1, 1, -2)]) for i, v in enumerate(back)]
    middle, late = [(up[3], both(0, -4))] + ahead[:-1] + back[:-1], [ahead[-1], back[-1]]
    state = work(early)
    near = jnp.concatenate([up[0][1:], down[0][1:], up[1][1:], down[1][1:]])
    far = jnp.concatenate([up[2][1:], down[2][1:], up[3][1:]])
    far, state = lax.optimization_barrier((far, state))
    for lump, dzs, n_right, n_left in ((near, (-1, 1, -2, 2), 1, 2), (far, (-3, 3, -4), 2, 1)):
        for step, n in ((1, n_right), (-1, n_left)):
            for i, v in enumerate(chain(lump, step, 0, n)):
                (middle if i == 0 else late).append((v, [(-step * (i + 1), dz, 1) for dz in dzs]))
    return state, middle, late


def attend_kernel(places, opening, closing, unroll, home_ref, bound_ref, q_ref, *refs):
    n_bufs = len(places)
    bufs, rest = refs[:n_bufs], refs[n_bufs:]
    if opening:
        inv, *rest = rest
    else:
        inv, rest = rest[0], rest[4:]
    m_ref, l_ref, acc_ref, *rest = rest
    if closing:
        o_ref, *rest = rest
    kv, lid, cnt, sem = rest
    me = lax.axis_index("ctx")
    my_x, my_z = me // NZ, me % NZ

    if opening:

        @pl.loop(0, NB)
        def _(b):
            inv[home_ref[b]] = b

        for qb in range(BPD):
            block = inv[me * BPD + qb]

            def earlier(i, first):
                at = block - 1 - i
                hit = (at >= 0) & (first < 0) & (bound_ref[jnp.maximum(at, 0)] < BLK)
                return jnp.where(hit, at, first)

            first = lax.fori_loop(0, BACK, earlier, jnp.int32(-1))
            first = jnp.where(bound_ref[block] == 0, block, jnp.maximum(first, 0))
            inv[NB + qb] = block
            inv[NB + BPD + qb] = first

    blocks = [inv[NB + qb] for qb in range(BPD)]
    firsts = [inv[NB + BPD + qb] for qb in range(BPD)]
    for qb in range(BPD):
        cnt[qb] = 0

    def fetch(src, qb, slot):
        return pltpu.make_async_copy(src, kv.at[qb, slot], sem.at[qb, slot])

    def list_slot(qb, logical):
        slot = cnt[qb]
        lid[qb, slot] = logical
        cnt[qb] = slot + 1
        return slot

    if opening:
        for qb in range(BPD):
            fetch(bufs[0].at[qb], qb, list_slot(qb, blocks[qb])).start()

    for buf, spots in zip(bufs, places):
        for i, (dx, dz, b) in enumerate(spots):
            stored = ((my_x + dx + NX) % NX * NZ + (my_z + dz + NZ) % NZ) * BPD + b
            logical = inv[stored]
            for qb in range(BPD):

                @pl.when((logical >= firsts[qb]) & (logical < blocks[qb]))
                def _():
                    fetch(buf.at[i], qb, list_slot(qb, logical)).start()

    @pl.loop(0, BPD)
    def _(qb):
        block, first = inv[NB + qb], inv[NB + BPD + qb]
        top_row = pl.multiple_of(qb * BLK, BLK)
        bound = bound_ref[block]
        first_bound = bound_ref[first]
        doc_start = first * BLK + jnp.where((first < block) & (first_bound < BLK), first_bound, 0)
        row = lax.broadcasted_iota(jnp.int32, (BLK, 1), 0)
        low = jnp.where(row < bound, doc_start, block * BLK + bound)
        high = row + block * BLK

        def allowed(ids):
            col = lax.broadcasted_iota(jnp.int32, (1, BLK), 1)
            at = jnp.concatenate([col + i * BLK for i in ids], 1)
            return (at >= low) & (at <= high)

        def step(slots, ids, masked, fresh):
            keys = jnp.concatenate([kv[qb, s, :, 0].reshape(BLK, HEAD_DIM) for s in slots])
            vals = jnp.concatenate([kv[qb, s, :, 1].reshape(BLK, HEAD_DIM) for s in slots])
            n = len(slots) * BLK // HEAD_DIM
            vals = jnp.concatenate([vals, jnp.ones_like(vals)], 1)
            mask = allowed(ids) if masked else None

            def one_head(h):
                lanes = pl.ds(pl.multiple_of(h * HEAD_DIM, HEAD_DIM), HEAD_DIM)
                for r in range(0, BLK, RT):
                    at = (qb * GROUP + h, pl.ds(r, RT))
                    q = q_ref[pl.ds(top_row + r, RT), lanes]
                    s = lax.dot_general(
                        q, keys, (((1,), (1,)), ((), ())), preferred_element_type=jnp.float32
                    )
                    s = s * SCALE
                    if masked:
                        s = jnp.where(mask[r : r + RT], s, NEG)
                    top = jnp.max(s, axis=1, keepdims=True)
                    if fresh:
                        top = jnp.broadcast_to(top, (RT, HEAD_DIM))
                    else:
                        before = m_ref[at]
                        top = jnp.maximum(before, top)
                        fade = jnp.exp2(before - top)
                    w = jnp.exp2(s - jnp.concatenate([top] * n, 1))
                    pv = jnp.dot(
                        w.astype(jnp.bfloat16), vals, preferred_element_type=jnp.float32
                    )
                    m_ref[at] = top
                    if fresh:
                        l_ref[at] = pv[:, HEAD_DIM:]
                        acc_ref[at] = pv[:, :HEAD_DIM]
                    else:
                        l_ref[at] = l_ref[at] * fade + pv[:, HEAD_DIM:]
                        acc_ref[at] = acc_ref[at] * fade + pv[:, :HEAD_DIM]

            if unroll == GROUP:
                for h in range(GROUP):
                    one_head(h)
            else:

                @pl.loop(0, GROUP // unroll)
                def _(g):
                    for i in range(unroll):
                        one_head(g * unroll + i)

        def arrived(slot):
            fetch(bufs[0].at[0], qb, slot).wait()

        if opening:
            arrived(0)
            step([0], [block], True, True)
            base = 1
        else:
            base = 0
        seen = cnt[qb] - base

        @pl.loop(0, seen // 2)
        def _(c):
            slots = [base + 2 * c, base + 1 + 2 * c]
            for s in slots:
                arrived(s)
            ids = [lid[qb, s] for s in slots]
            edge = (bound < BLK) | (ids[0] == first) | (ids[1] == first)

            @pl.when(edge)
            def _():
                step(slots, ids, True, False)

            @pl.when(jnp.logical_not(edge))
            def _():
                step(slots, ids, False, False)

        @pl.when(seen % 2 == 1)
        def _():
            last = base + seen - 1
            arrived(last)
            step([last], [lid[qb, last]], True, False)

        if closing:
            for h in range(GROUP):
                at = qb * GROUP + h
                o_ref[pl.ds(top_row, BLK), h * HEAD_DIM : (h + 1) * HEAD_DIM] = (
                    acc_ref[at] / l_ref[at]
                ).astype(o_ref.dtype)


def attend(queries, block_bound, block_home, pieces, state=(), closing=True, unroll=UNROLL):
    bufs = [v for v, _ in pieces]
    places = [p for _, p in pieces]
    smem = pl.BlockSpec(memory_space=pltpu.SMEM)
    vmem = pl.BlockSpec(memory_space=pltpu.VMEM)
    stat = (BPD * GROUP, BLK, HEAD_DIM)
    n_blocks = sum(len(p) for p in places)
    out_shape = [jax.ShapeDtypeStruct(stat, jnp.float32)] * 3
    out_specs = [vmem] * 3
    table = [jax.ShapeDtypeStruct((NB + 2 * BPD,), jnp.int32)]
    if not state:
        out_shape, out_specs = table + out_shape, [smem] + out_specs
    if closing:
        out_shape = out_shape + [jax.ShapeDtypeStruct(queries.shape, queries.dtype)]
        out_specs = out_specs + [vmem]
    n_in = 3 + len(bufs)
    out = pl.pallas_call(
        functools.partial(attend_kernel, places, not state, closing, unroll),
        out_shape=out_shape,
        in_specs=[smem, smem, vmem]
        + [pl.BlockSpec(memory_space=pl.ANY)] * len(bufs)
        + ([smem] + [vmem] * 3 if state else []),
        out_specs=out_specs,
        input_output_aliases={n_in + 1 + i: i for i in range(3)} if state else {},
        scratch_shapes=[
            pltpu.VMEM((BPD, BACK, 4, 2, 64, HEAD_DIM), jnp.bfloat16),
            pltpu.SMEM((BPD, BACK), jnp.int32),
            pltpu.SMEM((BPD,), jnp.int32),
            pltpu.SemaphoreType.DMA((BPD, BACK)),
        ],
        cost_estimate=pl.CostEstimate(
            flops=n_blocks * COST, bytes_accessed=8 * 1024 * 1024, transcendentals=0
        ),
        compiler_params=pltpu.CompilerParams(vmem_limit_bytes=32 * 1024 * 1024),
    )(block_home, block_bound, queries, *bufs, *state)
    if closing:
        return out[-1]
    return out if not state else [state[0], *out]


def on_device(queries, keys, values, block_bound, block_home, pair_query, pair_key):
    rows = keys.shape[0]
    heads = keys.shape[1] // HEAD_DIM
    own = lax.all_to_all(
        jnp.concatenate([keys, values]), "tp", split_axis=1, concat_axis=0, tiled=True
    )
    own = own.reshape(BPD, heads // BPD, 2, rows, HEAD_DIM)
    args = (queries, block_bound, block_home)
    state, middle, late = gather_blocks(own, lambda pieces: attend(*args, pieces, closing=False))
    state = attend(*args, middle, state, closing=False)
    return attend(*args, late, state)


def solution(mesh):
    in_specs = (
        P("ctx", "tp"),
        P(("ctx", "tp"), None),
        P(("ctx", "tp"), None),
        P(),
        P(),
        P("ctx", None),
        P("ctx", None),
    )
    return jax.shard_map(
        on_device, mesh=mesh, in_specs=in_specs, out_specs=P("ctx", "tp"), check_vma=False
    )
```

```python
import functools

import jax
import jax.numpy as jnp
from jax import lax
from jax.experimental import pallas as pl
from jax.experimental.pallas import tpu as pltpu
from jax.sharding import PartitionSpec as P

HEAD_DIM = 128
BLK = 256
BPD = 2
NB = 64
GROUP = 8
NX, NZ = 4, 8
BACK = 16
NEG = -1e30
RT = 128
UNROLL = 8
COST = 300 * 1000 * 1000
SCALE = HEAD_DIM ** (-0.5) * 1.4426950408889634


def moved(block, dx, dz):
    route = [
        (x * NZ + z, (x + dx) % NX * NZ + (z + dz) % NZ)
        for x in range(NX)
        for z in range(NZ)
    ]
    return lax.ppermute(block, "ctx", route)


def chain(block, dx, dz, steps):
    out = []
    for _ in range(steps):
        block = moved(block, dx, dz)
        out.append(block)
    return out


def gather_blocks(own, work):
    up = chain(own, 0, 1, 3)
    down = chain(own, 0, -1, 4)
    right = chain(own, 1, 0, 2)
    left = chain(own, -1, 0, 1)
    both = lambda dx, dz: [(dx, dz, 0), (dx, dz, 1)]
    early = [(own, both(0, 0))]
    early += [(v, both(0, -i - 1)) for i, v in enumerate(up)]
    early += [(v, both(0, i + 1)) for i, v in enumerate(down[:3])]
    early += [(v, both(-i - 1, 0)) for i, v in enumerate(right)]
    early += [(v, both(i + 1, 0)) for i, v in enumerate(left)]
    first = jnp.concatenate([right[0][:1], left[0][:1], right[1][:1]])
    ahead = chain(first, 0, 1, 4)
    back = chain(first, 0, -1, 3)
    ahead = [(v, [(dx, -i - 1, 0) for dx in (-1, 1, -2)]) for i, v in enumerate(ahead)]
    back = [(v, [(dx, i + 1, 0) for dx in (-1, 1, -2)]) for i, v in enumerate(back)]
    middle, late = [(down[3], both(0, 4))] + ahead[:-1] + back[:-1], [ahead[-1], back[-1]]
    state = work(early)
    near = jnp.concatenate([up[0][1:], down[0][1:], up[1][1:], down[1][1:]])
    far = jnp.concatenate([up[2][1:], down[2][1:], down[3][1:]])
    far, state = lax.optimization_barrier((far, state))
    for lump, dzs, n_right, n_left in ((near, (-1, 1, -2, 2), 1, 2), (far, (-3, 3, 4), 2, 1)):
        for step, n in ((1, n_right), (-1, n_left)):
            for i, v in enumerate(chain(lump, step, 0, n)):
                hop_on = i + 1 < n or (n == 1 and len(dzs) == 4)
                (middle if hop_on else late).append((v, [(-step * (i + 1), dz, 1) for dz in dzs]))
    return state, middle, late


def attend_kernel(places, opening, closing, unroll, home_ref, bound_ref, q_ref, *refs):
    n_bufs = len(places)
    bufs, rest = refs[:n_bufs], refs[n_bufs:]
    if opening:
        inv, *rest = rest
    else:
        inv, rest = rest[0], rest[4:]
    m_ref, l_ref, acc_ref, *rest = rest
    if closing:
        o_ref, *rest = rest
    kv, lid, cnt, sem = rest
    me = lax.axis_index("ctx")
    my_x, my_z = me // NZ, me & (NZ - 1)
    of_x = {dx: ((my_x + dx) & (NX - 1)) * (NZ * BPD) for dx in (-2, -1, 0, 1, 2)}
    of_z = {dz: ((my_z + dz) & (NZ - 1)) * BPD for dz in range(-4, 5)}

    if opening:

        @pl.loop(0, NB)
        def _(b):
            inv[home_ref[b]] = b

        for qb in range(BPD):
            block = inv[me * BPD + qb]

            def earlier(i, first):
                at = block - 1 - i
                hit = (at >= 0) & (first < 0) & (bound_ref[jnp.maximum(at, 0)] < BLK)
                return jnp.where(hit, at, first)

            first = lax.fori_loop(0, BACK, earlier, jnp.int32(-1))
            first = jnp.where(bound_ref[block] == 0, block, jnp.maximum(first, 0))
            inv[NB + qb] = block
            inv[NB + BPD + qb] = first

    blocks = [inv[NB + qb] for qb in range(BPD)]
    firsts = [inv[NB + BPD + qb] for qb in range(BPD)]
    for qb in range(BPD):
        cnt[qb] = 0

    def fetch(src, qb, slot):
        return pltpu.make_async_copy(src, kv.at[qb, slot], sem.at[qb, slot])

    def list_slot(qb, logical):
        slot = cnt[qb]
        lid[qb, slot] = logical
        cnt[qb] = slot + 1
        return slot

    if opening:
        for qb in range(BPD):
            fetch(bufs[0].at[qb], qb, list_slot(qb, blocks[qb])).start()

    for buf, spots in zip(bufs, places):
        for i, (dx, dz, b) in enumerate(spots):
            logical = inv[of_x[dx] + of_z[dz] + b]
            for qb in range(BPD):

                @pl.when((logical >= firsts[qb]) & (logical < blocks[qb]))
                def _():
                    fetch(buf.at[i], qb, list_slot(qb, logical)).start()

    @pl.loop(0, BPD)
    def _(qb):
        block, first = inv[NB + qb], inv[NB + BPD + qb]
        top_row = pl.multiple_of(qb * BLK, BLK)
        bound = bound_ref[block]
        first_bound = bound_ref[first]
        doc_start = first * BLK + jnp.where((first < block) & (first_bound < BLK), first_bound, 0)
        row = lax.broadcasted_iota(jnp.int32, (BLK, 1), 0)
        low = jnp.where(row < bound, doc_start, block * BLK + bound)
        high = row + block * BLK

        def allowed(ids):
            col = lax.broadcasted_iota(jnp.int32, (1, BLK), 1)
            at = jnp.concatenate([col + i * BLK for i in ids], 1)
            return (at >= low) & (at <= high)

        def step(slots, ids, masked, fresh):
            keys = jnp.concatenate([kv[qb, s, :, 0].reshape(BLK, HEAD_DIM) for s in slots])
            vals = jnp.concatenate([kv[qb, s, :, 1].reshape(BLK, HEAD_DIM) for s in slots])
            n = len(slots) * BLK // HEAD_DIM
            vals = jnp.concatenate([vals, jnp.ones_like(vals)], 1)
            mask = allowed(ids) if masked else None

            def one_head(h):
                lanes = pl.ds(pl.multiple_of(h * HEAD_DIM, HEAD_DIM), HEAD_DIM)
                for r in range(0, BLK, RT):
                    at = (qb * GROUP + h, pl.ds(r, RT))
                    q = q_ref[pl.ds(top_row + r, RT), lanes]
                    s = lax.dot_general(
                        q, keys, (((1,), (1,)), ((), ())), preferred_element_type=jnp.float32
                    )
                    if masked:
                        s = jnp.where(mask[r : r + RT], s, NEG)
                    top = jnp.max(s, axis=1, keepdims=True)
                    if fresh:
                        top = jnp.broadcast_to(top, (RT, HEAD_DIM))
                    else:
                        before = m_ref[at]
                        top = jnp.maximum(before, top)
                        fade = jnp.exp2((before - top) * SCALE)
                    w = jnp.exp2((s - jnp.concatenate([top] * n, 1)) * SCALE)
                    pv = jnp.dot(
                        w.astype(jnp.bfloat16), vals, preferred_element_type=jnp.float32
                    )
                    m_ref[at] = top
                    if fresh:
                        l_ref[at] = pv[:, HEAD_DIM:]
                        acc_ref[at] = pv[:, :HEAD_DIM]
                    else:
                        l_ref[at] = l_ref[at] * fade + pv[:, HEAD_DIM:]
                        acc_ref[at] = acc_ref[at] * fade + pv[:, :HEAD_DIM]

            if unroll == GROUP:
                for h in range(GROUP):
                    one_head(h)
            else:

                @pl.loop(0, GROUP // unroll)
                def _(g):
                    for i in range(unroll):
                        one_head(g * unroll + i)

        def arrived(slot):
            fetch(bufs[0].at[0], qb, slot).wait()

        if opening:
            arrived(0)
            step([0], [block], True, True)
            base = 1
        else:
            base = 0
        seen = cnt[qb] - base

        @pl.loop(0, seen // 2)
        def _(c):
            slots = [base + 2 * c, base + 1 + 2 * c]
            for s in slots:
                arrived(s)
            ids = [lid[qb, s] for s in slots]
            edge = (bound < BLK) | (ids[0] == first) | (ids[1] == first)

            @pl.when(edge)
            def _():
                step(slots, ids, True, False)

            @pl.when(jnp.logical_not(edge))
            def _():
                step(slots, ids, False, False)

        @pl.when(seen % 2 == 1)
        def _():
            last = base + seen - 1
            arrived(last)
            step([last], [lid[qb, last]], True, False)

        if closing:
            for h in range(GROUP):
                at = qb * GROUP + h
                o_ref[pl.ds(top_row, BLK), h * HEAD_DIM : (h + 1) * HEAD_DIM] = (
                    acc_ref[at] / l_ref[at]
                ).astype(o_ref.dtype)


def attend(queries, block_bound, block_home, pieces, state=(), closing=True, unroll=UNROLL):
    bufs = [v for v, _ in pieces]
    places = [p for _, p in pieces]
    smem = pl.BlockSpec(memory_space=pltpu.SMEM)
    vmem = pl.BlockSpec(memory_space=pltpu.VMEM)
    stat = (BPD * GROUP, BLK, HEAD_DIM)
    n_blocks = sum(len(p) for p in places)
    out_shape = [jax.ShapeDtypeStruct(stat, jnp.float32)] * 3
    out_specs = [vmem] * 3
    table = [jax.ShapeDtypeStruct((NB + 2 * BPD,), jnp.int32)]
    if not state:
        out_shape, out_specs = table + out_shape, [smem] + out_specs
    if closing:
        out_shape = out_shape + [jax.ShapeDtypeStruct(queries.shape, queries.dtype)]
        out_specs = out_specs + [vmem]
    n_in = 3 + len(bufs)
    out = pl.pallas_call(
        functools.partial(attend_kernel, places, not state, closing, unroll),
        out_shape=out_shape,
        in_specs=[smem, smem, vmem]
        + [pl.BlockSpec(memory_space=pl.ANY)] * len(bufs)
        + ([smem] + [vmem] * 3 if state else []),
        out_specs=out_specs,
        input_output_aliases={n_in + 1 + i: i for i in range(3)} if state else {},
        scratch_shapes=[
            pltpu.VMEM((BPD, BACK, 4, 2, 64, HEAD_DIM), jnp.bfloat16),
            pltpu.SMEM((BPD, BACK), jnp.int32),
            pltpu.SMEM((BPD,), jnp.int32),
            pltpu.SemaphoreType.DMA((BPD, BACK)),
        ],
        cost_estimate=pl.CostEstimate(
            flops=n_blocks * COST, bytes_accessed=8 * 1024 * 1024, transcendentals=0
        ),
        compiler_params=pltpu.CompilerParams(vmem_limit_bytes=32 * 1024 * 1024),
    )(block_home, block_bound, queries, *bufs, *state)
    if closing:
        return out[-1]
    return out if not state else [state[0], *out]


def on_device(queries, keys, values, block_bound, block_home, pair_query, pair_key):
    rows = keys.shape[0]
    heads = keys.shape[1] // HEAD_DIM
    own = lax.all_to_all(
        jnp.concatenate([keys, values]), "tp", split_axis=1, concat_axis=0, tiled=True
    )
    own = own.reshape(BPD, heads // BPD, 2, rows, HEAD_DIM)
    args = (queries, block_bound, block_home)
    state, middle, late = gather_blocks(own, lambda pieces: attend(*args, pieces, closing=False))
    state = attend(*args, middle, state, closing=False)
    return attend(*args, late, state)


def solution(mesh):
    in_specs = (
        P("ctx", "tp"),
        P(("ctx", "tp"), None),
        P(("ctx", "tp"), None),
        P(),
        P(),
        P("ctx", None),
        P("ctx", None),
    )
    return jax.shard_map(
        on_device, mesh=mesh, in_specs=in_specs, out_specs=P("ctx", "tp"), check_vma=False
    )
```

```python
import functools

import jax
import jax.numpy as jnp
from jax import lax
from jax.experimental import pallas as pl
from jax.experimental.pallas import tpu as pltpu
from jax.sharding import PartitionSpec as P

HEAD_DIM = 128
BLK = 256
BPD = 2
NB = 64
GROUP = 8
NX, NZ = 4, 8
BACK = 16
NEG = -1e30
RT = 128
UNROLL = 8
COST = 300 * 1000 * 1000
SCALE = HEAD_DIM ** (-0.5) * 1.4426950408889634


def moved(block, dx, dz):
    route = [
        (x * NZ + z, (x + dx) % NX * NZ + (z + dz) % NZ)
        for x in range(NX)
        for z in range(NZ)
    ]
    return lax.ppermute(block, "ctx", route)


def chain(block, dx, dz, steps):
    out = []
    for _ in range(steps):
        block = moved(block, dx, dz)
        out.append(block)
    return out


def gather_blocks(own, work):
    up = chain(own, 0, 1, 3)
    down = chain(own, 0, -1, 4)
    right = chain(own, 1, 0, 2)
    left = chain(own, -1, 0, 1)
    both = lambda dx, dz: [(dx, dz, 0), (dx, dz, 1)]
    early = [(own, both(0, 0))]
    early += [(v, both(0, -i - 1)) for i, v in enumerate(up)]
    early += [(v, both(0, i + 1)) for i, v in enumerate(down[:3])]
    early += [(v, both(-i - 1, 0)) for i, v in enumerate(right)]
    early += [(v, both(i + 1, 0)) for i, v in enumerate(left)]
    first = jnp.concatenate([right[0][:1], left[0][:1], right[1][:1]])
    ahead = chain(first, 0, 1, 4)
    back = chain(first, 0, -1, 3)
    ahead = [(v, [(dx, -i - 1, 0) for dx in (-1, 1, -2)]) for i, v in enumerate(ahead)]
    back = [(v, [(dx, i + 1, 0) for dx in (-1, 1, -2)]) for i, v in enumerate(back)]
    middle, late = [(down[3], both(0, 4))] + ahead[:-1] + back[:-1], [ahead[-1], back[-1]]
    state = work(early)
    near = jnp.concatenate([up[0][1:], down[0][1:], up[1][1:], down[1][1:]])
    far = jnp.concatenate([up[2][1:], down[2][1:], down[3][1:]])
    far, state = lax.optimization_barrier((far, state))
    for lump, dzs, n_right, n_left in ((near, (-1, 1, -2, 2), 1, 2), (far, (-3, 3, 4), 2, 1)):
        for step, n in ((1, n_right), (-1, n_left)):
            for i, v in enumerate(chain(lump, step, 0, n)):
                hop_on = i + 1 < n or (n == 1 and len(dzs) == 4)
                (middle if hop_on else late).append((v, [(-step * (i + 1), dz, 1) for dz in dzs]))
    return state, middle, late


def attend_kernel(places, opening, closing, unroll, home_ref, bound_ref, q_ref, *refs):
    n_bufs = len(places)
    bufs, rest = refs[:n_bufs], refs[n_bufs:]
    if opening:
        inv, *rest = rest
    else:
        inv, rest = rest[0], rest[4:]
    m_ref, l_ref, acc_ref, *rest = rest
    if closing:
        o_ref, *rest = rest
    kv, lid, cnt, sem = rest
    me = lax.axis_index("ctx")
    my_x, my_z = me // NZ, me & (NZ - 1)
    of_x = {dx: ((my_x + dx) & (NX - 1)) * (NZ * BPD) for dx in (-2, -1, 0, 1, 2)}
    of_z = {dz: ((my_z + dz) & (NZ - 1)) * BPD for dz in range(-4, 5)}

    if opening:

        @pl.loop(0, NB)
        def _(b):
            inv[home_ref[b]] = b

        for qb in range(BPD):
            block = inv[me * BPD + qb]

            def earlier(i, first):
                at = block - 1 - i
                hit = (at >= 0) & (first < 0) & (bound_ref[jnp.maximum(at, 0)] < BLK)
                return jnp.where(hit, at, first)

            first = lax.fori_loop(0, BACK, earlier, jnp.int32(-1))
            first = jnp.where(bound_ref[block] == 0, block, jnp.maximum(first, 0))
            inv[NB + qb] = block
            inv[NB + BPD + qb] = first

    blocks = [inv[NB + qb] for qb in range(BPD)]
    firsts = [inv[NB + BPD + qb] for qb in range(BPD)]
    for qb in range(BPD):
        cnt[qb] = 0

    def fetch(src, qb, slot):
        return pltpu.make_async_copy(src, kv.at[qb, slot], sem.at[qb, slot])

    def list_slot(qb, logical):
        slot = cnt[qb]
        lid[qb, slot] = logical
        cnt[qb] = slot + 1
        return slot

    if opening:
        for qb in range(BPD):
            fetch(bufs[0].at[qb], qb, list_slot(qb, blocks[qb])).start()

    for buf, spots in zip(bufs, places):
        for i, (dx, dz, b) in enumerate(spots):
            logical = inv[of_x[dx] + of_z[dz] + b]
            for qb in range(BPD):

                @pl.when((logical >= firsts[qb]) & (logical < blocks[qb]))
                def _():
                    fetch(buf.at[i], qb, list_slot(qb, logical)).start()

    @pl.loop(0, BPD)
    def _(qb):
        block, first = inv[NB + qb], inv[NB + BPD + qb]
        top_row = pl.multiple_of(qb * BLK, BLK)
        bound = bound_ref[block]
        first_bound = bound_ref[first]
        doc_start = first * BLK + jnp.where((first < block) & (first_bound < BLK), first_bound, 0)
        row = lax.broadcasted_iota(jnp.int32, (BLK, 1), 0)
        low = jnp.where(row < bound, doc_start, block * BLK + bound)
        high = row + block * BLK

        def allowed(ids):
            col = lax.broadcasted_iota(jnp.int32, (1, BLK), 1)
            at = jnp.concatenate([col + i * BLK for i in ids], 1)
            return (at >= low) & (at <= high)

        def step(slots, ids, masked, fresh):
            keys = jnp.concatenate([kv[qb, s, :, 0].reshape(BLK, HEAD_DIM) for s in slots])
            vals = jnp.concatenate([kv[qb, s, :, 1].reshape(BLK, HEAD_DIM) for s in slots])
            n = len(slots) * BLK // HEAD_DIM
            vals = jnp.concatenate([vals, jnp.ones_like(vals)], 1)
            mask = allowed(ids) if masked else None

            def one_head(h):
                lanes = pl.ds(pl.multiple_of(h * HEAD_DIM, HEAD_DIM), HEAD_DIM)
                for r in range(0, BLK, RT):
                    at = (qb * GROUP + h, pl.ds(r, RT))
                    q = q_ref[pl.ds(top_row + r, RT), lanes]
                    s = lax.dot_general(
                        q, keys, (((1,), (1,)), ((), ())), preferred_element_type=jnp.float32
                    )
                    if masked:
                        s = jnp.where(mask[r : r + RT], s, NEG)
                    top = jnp.max(s, axis=1, keepdims=True)
                    if fresh:
                        top = jnp.broadcast_to(top, (RT, HEAD_DIM))
                    else:
                        before = m_ref[at]
                        top = jnp.maximum(before, top)
                        fade = jnp.exp2((before - top) * SCALE)
                    w = jnp.exp2((s - jnp.concatenate([top] * n, 1)) * SCALE)
                    pv = jnp.dot(
                        w.astype(jnp.bfloat16), vals, preferred_element_type=jnp.float32
                    )
                    m_ref[at] = top
                    if fresh:
                        l_ref[at] = pv[:, HEAD_DIM:]
                        acc_ref[at] = pv[:, :HEAD_DIM]
                    else:
                        l_ref[at] = l_ref[at] * fade + pv[:, HEAD_DIM:]
                        acc_ref[at] = acc_ref[at] * fade + pv[:, :HEAD_DIM]

            if unroll == GROUP:
                for h in range(GROUP):
                    one_head(h)
            else:

                @pl.loop(0, GROUP // unroll)
                def _(g):
                    for i in range(unroll):
                        one_head(g * unroll + i)

        def arrived(slot):
            fetch(bufs[0].at[0], qb, slot).wait()

        if opening:
            odd = (cnt[qb] - 1) % 2
            arrived(0)

            @pl.when(odd == 0)
            def _():
                step([0], [block], True, True)

            @pl.when(odd == 1)
            def _():
                arrived(1)
                step([0, 1], [block, lid[qb, 1]], True, True)

            base = 1 + odd
        else:
            base = 0
        seen = cnt[qb] - base

        @pl.loop(0, seen // 2)
        def _(c):
            slots = [base + 2 * c, base + 1 + 2 * c]
            for s in slots:
                arrived(s)
            ids = [lid[qb, s] for s in slots]
            edge = (bound < BLK) | (ids[0] == first) | (ids[1] == first)

            @pl.when(edge)
            def _():
                step(slots, ids, True, False)

            @pl.when(jnp.logical_not(edge))
            def _():
                step(slots, ids, False, False)

        if not opening:

            @pl.when(seen % 2 == 1)
            def _():
                last = base + seen - 1
                arrived(last)
                step([last], [lid[qb, last]], True, False)

        if closing:
            for h in range(GROUP):
                at = qb * GROUP + h
                o_ref[pl.ds(top_row, BLK), h * HEAD_DIM : (h + 1) * HEAD_DIM] = (
                    acc_ref[at] / l_ref[at]
                ).astype(o_ref.dtype)


def attend(queries, block_bound, block_home, pieces, state=(), closing=True, unroll=UNROLL):
    bufs = [v for v, _ in pieces]
    places = [p for _, p in pieces]
    smem = pl.BlockSpec(memory_space=pltpu.SMEM)
    vmem = pl.BlockSpec(memory_space=pltpu.VMEM)
    stat = (BPD * GROUP, BLK, HEAD_DIM)
    n_blocks = sum(len(p) for p in places)
    out_shape = [jax.ShapeDtypeStruct(stat, jnp.float32)] * 3
    out_specs = [vmem] * 3
    table = [jax.ShapeDtypeStruct((NB + 2 * BPD,), jnp.int32)]
    if not state:
        out_shape, out_specs = table + out_shape, [smem] + out_specs
    if closing:
        out_shape = out_shape + [jax.ShapeDtypeStruct(queries.shape, queries.dtype)]
        out_specs = out_specs + [vmem]
    n_in = 3 + len(bufs)
    out = pl.pallas_call(
        functools.partial(attend_kernel, places, not state, closing, unroll),
        out_shape=out_shape,
        in_specs=[smem, smem, vmem]
        + [pl.BlockSpec(memory_space=pl.ANY)] * len(bufs)
        + ([smem] + [vmem] * 3 if state else []),
        out_specs=out_specs,
        input_output_aliases={n_in + 1 + i: i for i in range(3)} if state else {},
        scratch_shapes=[
            pltpu.VMEM((BPD, BACK, 4, 2, 64, HEAD_DIM), jnp.bfloat16),
            pltpu.SMEM((BPD, BACK), jnp.int32),
            pltpu.SMEM((BPD,), jnp.int32),
            pltpu.SemaphoreType.DMA((BPD, BACK)),
        ],
        cost_estimate=pl.CostEstimate(
            flops=n_blocks * COST, bytes_accessed=8 * 1024 * 1024, transcendentals=0
        ),
        compiler_params=pltpu.CompilerParams(vmem_limit_bytes=32 * 1024 * 1024),
    )(block_home, block_bound, queries, *bufs, *state)
    if closing:
        return out[-1]
    return out if not state else [state[0], *out]


def on_device(queries, keys, values, block_bound, block_home, pair_query, pair_key):
    rows = keys.shape[0]
    heads = keys.shape[1] // HEAD_DIM
    own = lax.all_to_all(
        jnp.concatenate([keys, values]), "tp", split_axis=1, concat_axis=0, tiled=True
    )
    own = own.reshape(BPD, heads // BPD, 2, rows, HEAD_DIM)
    args = (queries, block_bound, block_home)
    state, middle, late = gather_blocks(own, lambda pieces: attend(*args, pieces, closing=False))
    state = attend(*args, middle, state, closing=False)
    return attend(*args, late, state)


def solution(mesh):
    in_specs = (
        P("ctx", "tp"),
        P(("ctx", "tp"), None),
        P(("ctx", "tp"), None),
        P(),
        P(),
        P("ctx", None),
        P("ctx", None),
    )
    return jax.shard_map(
        on_device, mesh=mesh, in_specs=in_specs, out_specs=P("ctx", "tp"), check_vma=False
    )
```
